32 devices in a mesh: groups: 2 (over y), row: 4 (over z), col: 4 (over x, core).
Axes of the slice: x: 2, y: 2, z: 4, core: 2. Of those that a mesh axis runs over, the one named last changes fastest.
Arguments:
- forward: bfloat16 [32768, 1024], P(('groups', 'row', 'col')), parts along dimension 0, may hold values from 0.049804688 to 1
- adjoint: bfloat16 [32768, 1024], P(('groups', 'col', 'row')), parts along dimension 0, may hold values from 0.049804688 to 1
- emission: bfloat16 [16384, 256], P(('col', 'row')), may hold values from 0.0099487305 to 1
- emit_index: int32 [2048], P('groups'), parts along dimension 0, may hold values from 0 to 255
- transition: bfloat16 [16384, 16384], P('row', 'col'), may hold values from 0.02 to 30
Outputs:
- updated: bfloat16 [32768, 16384], P(('groups', 'row'), 'col'), parts along dimension 0
The draws below stay inside these ranges and needn't reach their ends.
There are 2 independent parts, one for each index of `groups`. The reference program is written for one: setup_inputs(seed, part) draws one part's arguments, and reference() takes and returns one part's arrays. A program takes and returns all parts, laid end to end along the dimension named above; an argument that names none is the same for every part. Nothing has to cross between parts.
All inputs are finite; a program needn't handle non-finite values.
Results may differ from the reference program's by a relative error of at most 0.0034.
Values may be sent and summed in bfloat16 or wider, within the bound.
A program may use at most 320 MiB of HBM per device.

```python
import math
import jax
import jax.numpy as jnp
from jax import lax

STATES = 16384
POSITIONS = 1024
SYMBOLS = 256


def draw_transition(key, part):
    key = jax.random.fold_in(key, 7)
    key_rough = jax.random.fold_in(key, 1)
    key_cols = jax.random.fold_in(key, 2)
    column = jnp.arange(STATES, dtype=jnp.float32)
    trend = math.log(3.0) * column / (STATES - 1)
    rough = jnp.exp(jax.random.uniform(key_rough, (STATES, STATES), jnp.float32, math.log(0.05), 0.0))
    expo = jax.random.uniform(key_cols, (STATES,), jnp.float32, 0.0, math.log(10.0))
    return (rough * jnp.exp(expo + trend)[None, :]).astype(jnp.bfloat16)


def set_ends(drawn, key, smallest, largest):
    extent = drawn.shape
    index_at = [jax.random.randint(jax.random.fold_in(key, axis), (), 0, extent[axis]) for axis in range(len(extent))]
    drawn = drawn.at[tuple(index_at)].set(smallest)
    longest = extent.index(max(extent))
    index_at[longest] = (index_at[longest] + 1) % extent[longest]
    return drawn.at[tuple(index_at)].set(largest)


def levels(key, extent, split, low, top_value):
    def one(axis_at, blocks):
        draws = jax.random.uniform(jax.random.fold_in(jax.random.fold_in(key, 6), axis_at), (blocks,), jnp.float32, low / len(split), top_value / len(split))
        return jnp.repeat(jnp.exp(draws), extent[axis_at] // blocks).reshape((-1,) + (1,) * (len(extent) - axis_at - 1))

    level = one(*split[0])
    for cut in split[1:]:
        level = level * one(*cut)
    return level


def setup_inputs(seed: int = 0, part: int = 0) -> dict:
    keys = jax.random.split(jax.random.key(seed), 6)
    part_keys = jax.random.split(jax.random.fold_in(keys[5], part), 6)
    forward = jnp.clip(jnp.exp(math.log(1.0) - 2.9996462 * jax.random.uniform(part_keys[0], (STATES, POSITIONS), jnp.float32) ** levels(part_keys[0], (STATES, POSITIONS), ((0, 16),), -0.2, 0.2)), 0.049804688, 1.0).astype(jnp.bfloat16)
    adjoint = jnp.clip(jnp.exp(math.log(1.0) - 2.9996462 * jax.random.uniform(part_keys[1], (STATES, POSITIONS), jnp.float32) ** levels(part_keys[1], (STATES, POSITIONS), ((0, 16),), -0.2, 0.2)), 0.049804688, 1.0).astype(jnp.bfloat16)
    emission = jnp.clip(jnp.exp(math.log(1.0) - 4.61031033 * jax.random.uniform(keys[2], (STATES, SYMBOLS), jnp.float32) ** levels(keys[2], (STATES, SYMBOLS), ((0, 16),), -0.2, 0.2)), 0.0099487305, 1.0).astype(jnp.bfloat16)
    emit_index = set_ends(jax.random.randint(part_keys[3], (POSITIONS,), 0, SYMBOLS), jax.random.fold_in(part_keys[3], 1), 0, SYMBOLS - 1).astype(jnp.int32)
    transition = draw_transition(jax.random.fold_in(keys[5], 71), part)
    return {"forward": forward, "adjoint": adjoint, "emission": emission, "emit_index": emit_index, "transition": transition}


def reference(forward, adjoint, emission, emit_index, transition):
    looked = emission[:, emit_index].astype(jnp.float32)
    weighted = (adjoint.astype(jnp.float32) * looked).astype(jnp.bfloat16)
    block_rows = 256
    fwd_blocks = forward.reshape(STATES // block_rows, block_rows, POSITIONS)
    trans_blocks = transition.reshape(STATES // block_rows, block_rows, STATES)

    def one_block(pair):
        fwd_rows, trans_rows = pair
        counts = jnp.dot(fwd_rows, weighted.T, preferred_element_type=jnp.float32)
        scaled = counts * trans_rows.astype(jnp.float32)
        total = jnp.sum(scaled, axis=1)
        return (scaled * (STATES / total)[:, None]).astype(jnp.bfloat16)

    updated = lax.map(one_block, (fwd_blocks, trans_blocks))
    return updated.reshape(STATES, STATES)
```

```python
import functools

import jax
import jax.numpy as jnp
from jax import lax
from jax.experimental import pallas as pl
from jax.experimental.pallas import tpu as pltpu
from jax.sharding import PartitionSpec as P

CHUNK = 256
ROWS = 512
MESH = pl.DeviceIdType.MESH


def kernel(n, m, states, idx_ref, em_ref, adj_ref, fwd_ref, trans_ref,
           scaled_ref, factor_ref,
           w, f, tbuf, obuf, acc, tot,
           w_recv, w_right, w_left, f_recv, f_right, f_left,
           t_sem, o_sem, tot_send, tot_recv, load_sem):
    groups = lax.axis_index("groups")
    p = lax.axis_index("row")
    c = lax.axis_index("col")
    shard = adj_ref.shape[0]
    chunks = shard // CHUNK
    rows = f.shape[0]
    symbols = em_ref.shape[1]
    positions = adj_ref.shape[1]

    def row_dev(q):
        return (groups, q, c)

    def col_dev(q):
        return (groups, p, q)

    def w_copy(i, sem, dev):
        return pltpu.make_async_remote_copy(
            src_ref=w.at[i], dst_ref=w.at[i], send_sem=sem.at[i], recv_sem=w_recv.at[i],
            device_id=row_dev(dev), device_id_type=MESH)

    def f_slice(i):
        return f.at[pl.ds(pl.multiple_of(i * CHUNK, CHUNK), CHUNK)]

    def f_copy(i, sem, dev):
        return pltpu.make_async_remote_copy(
            src_ref=f_slice(i), dst_ref=f_slice(i), send_sem=sem.at[i], recv_sem=f_recv.at[i],
            device_id=col_dev(dev), device_id_type=MESH)

    barrier = pltpu.get_barrier_semaphore()

    @pl.when(p > 0)
    def _():
        pl.semaphore_signal(barrier, inc=1, device_id=row_dev(p - 1), device_id_type=MESH)

    @pl.when(p < n - 1)
    def _():
        pl.semaphore_signal(barrier, inc=1, device_id=row_dev(p + 1), device_id_type=MESH)

    for step in range(1, m):
        pl.semaphore_signal(barrier, inc=1, device_id=col_dev(lax.rem(c + step, m)), device_id_type=MESH)

    load = pltpu.make_async_copy(fwd_ref, f.at[pl.ds(pl.multiple_of(c * shard, CHUNK), shard)], load_sem)
    load.start()

    def own_block(k):
        at = pl.ds(pl.multiple_of(k * CHUNK, CHUNK), CHUNK)
        one_hot = jnp.where(
            idx_ref[...] == lax.broadcasted_iota(jnp.int32, (symbols, positions), 0), 1.0, 0.0
        ).astype(jnp.bfloat16)
        looked = jnp.dot(em_ref[at, :], one_hot, preferred_element_type=jnp.float32)
        block = adj_ref[at, :].astype(jnp.float32) * looked
        w[p * chunks + k] = block.T.astype(jnp.bfloat16)

    own_block(0)
    pl.semaphore_wait(barrier, jnp.where(p > 0, 1, 0) + jnp.where(p < n - 1, 1, 0) + (m - 1))

    def send_own(k, _):
        @pl.when(k > 0)
        def _():
            own_block(k)

        i = p * chunks + k

        @pl.when(p > 0)
        def _():
            w_copy(i, w_left, p - 1).start()

        @pl.when(p < n - 1)
        def _():
            w_copy(i, w_right, p + 1).start()

        @pl.when(k == 0)
        def _():
            load.wait()

            def send_forward(kf, _):
                j = c * chunks + kf

                @pl.when(c > 0)
                def _():
                    f_copy(j, f_left, c - 1).start()

                @pl.when(c < m - 1)
                def _():
                    f_copy(j, f_right, c + 1).start()

                return 0

            lax.fori_loop(0, chunks, send_forward, 0)

        return 0

    lax.fori_loop(0, chunks, send_own, 0)

    def w_arrive(slot, k):
        i = slot * chunks + k

        @pl.when((slot >= 0) & (slot < n))
        def _():
            w_copy(i, w_left, p).wait_recv()

            @pl.when((slot < p) & (p < n - 1))
            def _():
                w_copy(i, w_right, p + 1).start()

            @pl.when((slot > p) & (p > 0))
            def _():
                w_copy(i, w_left, p - 1).start()

    def f_arrive(slot, k):
        i = slot * chunks + k

        @pl.when((slot >= 0) & (slot < m))
        def _():
            f_copy(i, f_left, c).wait_recv()

            @pl.when((slot < c) & (c < m - 1))
            def _():
                f_copy(i, f_right, c + 1).start()

            @pl.when((slot > c) & (c > 0))
            def _():
                f_copy(i, f_left, c - 1).start()

    def gather(step, _):
        d = 1 + step // chunks
        k = lax.rem(step, chunks)
        f_arrive(c - d, k)
        f_arrive(c + d, k)

        @pl.when(d == m - 1)
        def _():
            w_arrive(p - 1, k)
            w_arrive(p + 1, k)

        return 0

    acc[...] = jnp.zeros_like(acc)
    lax.fori_loop(0, (m - 1) * chunks, gather, 0)

    both = jnp.minimum(p, n - 1 - p)

    def slot_of(o):
        near = (o + 1) // 2
        near_slot = jnp.where(lax.rem(o, 2) == 1, p - near, p + near)
        far = o - both
        far_slot = jnp.where(p > n - 1 - p, p - far, p + far)
        return jnp.where(o <= 2 * both, near_slot, far_slot)

    def columns(q):
        i = slot_of(q // chunks) * chunks + lax.rem(q, chunks)
        return pl.ds(pl.multiple_of(i * CHUNK, CHUNK), CHUNK)

    def t_copy(q):
        b = lax.rem(q, 2)
        return pltpu.make_async_copy(trans_ref.at[:, columns(q)], tbuf.at[b], t_sem.at[b])

    def o_copy(q):
        b = lax.rem(q, 2)
        return pltpu.make_async_copy(obuf.at[b], scaled_ref.at[:, columns(q)], o_sem.at[b])

    t_copy(0).start()

    def block(q, _):
        slot = slot_of(q // chunks)
        k = lax.rem(q, chunks)
        b = lax.rem(q, 2)

        @pl.when(q + 1 < n * chunks)
        def _():
            t_copy(q + 1).start()

        @pl.when(jnp.abs(slot - p) > 1)
        def _():
            w_arrive(slot, k)

        @pl.when(q >= 2)
        def _():
            o_copy(q - 2).wait()

        t_copy(q).wait()
        i = slot * chunks + k

        def tile(r, _):
            at = pl.ds(pl.multiple_of(r * ROWS, ROWS), ROWS)
            counts = jnp.dot(f[at, :], w[i], preferred_element_type=jnp.float32)
            scaled = counts * tbuf[b, at, :].astype(jnp.float32)
            obuf[b, at, :] = scaled.astype(jnp.bfloat16)
            part = scaled[:, :128]
            for g in range(1, CHUNK // 128):
                part = part + scaled[:, g * 128:(g + 1) * 128]
            acc[at, :] += part
            return 0

        lax.fori_loop(0, rows // ROWS, tile, 0)
        o_copy(q).start()
        return 0

    lax.fori_loop(0, n * chunks, block, 0)

    def reduce(r, _):
        at = pl.ds(pl.multiple_of(r * ROWS, ROWS), ROWS)
        tot[c, :, at] = jnp.sum(acc[at, :].T, axis=0, keepdims=True)
        return 0

    lax.fori_loop(0, rows // ROWS, reduce, 0)

    def tot_copy(src, send, dev):
        return pltpu.make_async_remote_copy(
            src_ref=tot.at[src], dst_ref=tot.at[src], send_sem=tot_send.at[send], recv_sem=tot_recv.at[src],
            device_id=col_dev(dev), device_id_type=MESH)

    for step in range(1, m):
        tot_copy(c, step, lax.rem(c + step, m)).start()
    o_copy(n * chunks - 2).wait()
    o_copy(n * chunks - 1).wait()
    for step in range(1, m):
        tot_copy(lax.rem(c + step, m), step, c).wait_recv()
    factor_ref[...] = states / jnp.sum(tot[...], axis=0)
    for step in range(1, m):
        tot_copy(c, step, lax.rem(c + step, m)).wait_send()

    def sent(i, _):
        slot = i // chunks

        @pl.when((slot >= p) & (p > 0))
        def _():
            w_copy(i, w_left, p - 1).wait_send()

        @pl.when((slot <= p) & (p < n - 1))
        def _():
            w_copy(i, w_right, p + 1).wait_send()

        return 0

    lax.fori_loop(0, n * chunks, sent, 0)

    def f_sent(i, _):
        slot = i // chunks

        @pl.when((slot >= c) & (c > 0))
        def _():
            f_copy(i, f_left, c - 1).wait_send()

        @pl.when((slot <= c) & (c < m - 1))
        def _():
            f_copy(i, f_right, c + 1).wait_send()

        return 0

    lax.fori_loop(0, m * chunks, f_sent, 0)


def fused(n, m, forward, adjoint, emission, emit_index, transition):
    rows, cols = transition.shape
    shard, positions = forward.shape
    chunks = shard // CHUNK
    vmem = pl.BlockSpec(memory_space=pltpu.VMEM)
    anywhere = pl.BlockSpec(memory_space=pl.ANY)
    dma = pltpu.SemaphoreType.DMA
    scaled, factor = pl.pallas_call(
        functools.partial(kernel, n, m, float(cols * m)),
        out_shape=(
            jax.ShapeDtypeStruct((rows, cols), jnp.bfloat16),
            jax.ShapeDtypeStruct((1, rows), jnp.float32),
        ),
        in_specs=[vmem, vmem, vmem, anywhere, anywhere],
        out_specs=(anywhere, vmem),
        scratch_shapes=[
            pltpu.VMEM((n * chunks, positions, CHUNK), jnp.bfloat16),
            pltpu.VMEM((rows, positions), jnp.bfloat16),
            pltpu.VMEM((2, rows, CHUNK), jnp.bfloat16),
            pltpu.VMEM((2, rows, CHUNK), jnp.bfloat16),
            pltpu.VMEM((rows, 128), jnp.float32),
            pltpu.VMEM((m, 1, rows), jnp.float32),
            dma((n * chunks,)), dma((n * chunks,)), dma((n * chunks,)),
            dma((m * chunks,)), dma((m * chunks,)), dma((m * chunks,)),
            dma((2,)), dma((2,)), dma((m,)), dma((m,)), dma,
        ],
        compiler_params=pltpu.CompilerParams(
            collective_id=0, has_side_effects=True, vmem_limit_bytes=48 * 1024 * 1024),
        cost_estimate=pl.CostEstimate(
            flops=2 * rows * cols * positions, bytes_accessed=4 * rows * cols, transcendentals=0),
        name="counts_gather",
    )(emit_index.reshape(1, -1), emission, adjoint, forward, transition)
    return (scaled.astype(jnp.float32) * factor.reshape(rows, 1)).astype(jnp.bfloat16)


def plain(m, forward, adjoint, emission, emit_index, transition):
    symbols = emission.shape[1]
    one_hot = (emit_index[None, :] == lax.iota(jnp.int32, symbols)[:, None]).astype(jnp.bfloat16)
    looked = jnp.dot(emission, one_hot, preferred_element_type=jnp.float32)
    weighted = (adjoint.astype(jnp.float32) * looked).astype(jnp.bfloat16)
    sources = lax.all_gather(forward, "col", axis=0, tiled=True)
    targets = lax.all_gather(weighted, "row", axis=0, tiled=True)
    counts = lax.dot_general(sources, targets, (((1,), (1,)), ((), ())), preferred_element_type=jnp.float32)
    scaled = counts * transition.astype(jnp.float32)
    total = lax.psum(jnp.sum(scaled, axis=1), "col")
    return (scaled * (m * transition.shape[1] / total)[:, None]).astype(jnp.bfloat16)


def solution(mesh):
    n, m = mesh.shape["row"], mesh.shape["col"]

    def body(forward, adjoint, emission, emit_index, transition):
        args = (forward, adjoint, emission, emit_index, transition)
        if n > 2 and m > 1 and forward.shape[0] % CHUNK == 0:
            return fused(n, m, *args)
        return plain(m, *args)

    return jax.shard_map(
        body,
        mesh=mesh,
        in_specs=(
            P(("groups", "row", "col"), None),
            P(("groups", "col", "row"), None),
            P(("col", "row"), None),
            P("groups"),
            P("row", "col"),
        ),
        out_specs=P(("groups", "row"), "col"),
        check_vma=False,
    )
```

```python
import functools

import jax
import jax.numpy as jnp
from jax import lax
from jax.experimental import pallas as pl
from jax.experimental.pallas import tpu as pltpu
from jax.sharding import PartitionSpec as P

CHUNK = 256
ROWS = 512
MESH = pl.DeviceIdType.MESH


def kernel(n, m, states, idx_ref, em_ref, adj_ref, fwd_ref, trans_ref,
           scaled_ref, factor_ref,
           w, f, abuf, ebuf, tbuf, acc, tot,
           w_recv, w_right, w_left, f_recv, f_right, f_left,
           t_sem, a_sem, e_sem, tot_send, tot_recv, load_sem):
    groups = lax.axis_index("groups")
    p = lax.axis_index("row")
    c = lax.axis_index("col")
    shard = adj_ref.shape[0]
    chunks = shard // CHUNK
    rows = f.shape[0]
    symbols = em_ref.shape[1]
    positions = adj_ref.shape[1]

    def row_dev(q):
        return (groups, q, c)

    def col_dev(q):
        return (groups, p, q)

    def w_copy(i, sem, dev):
        return pltpu.make_async_remote_copy(
            src_ref=w.at[i], dst_ref=w.at[i], send_sem=sem.at[i], recv_sem=w_recv.at[i],
            device_id=row_dev(dev), device_id_type=MESH)

    def f_slice(i):
        return f.at[pl.ds(pl.multiple_of(i * CHUNK, CHUNK), CHUNK)]

    def f_copy(i, sem, dev):
        return pltpu.make_async_remote_copy(
            src_ref=f_slice(i), dst_ref=f_slice(i), send_sem=sem.at[i], recv_sem=f_recv.at[i],
            device_id=col_dev(dev), device_id_type=MESH)

    barrier = pltpu.get_barrier_semaphore()

    @pl.when(p > 0)
    def _():
        pl.semaphore_signal(barrier, inc=1, device_id=row_dev(p - 1), device_id_type=MESH)

    @pl.when(p < n - 1)
    def _():
        pl.semaphore_signal(barrier, inc=1, device_id=row_dev(p + 1), device_id_type=MESH)

    for step in range(1, m):
        pl.semaphore_signal(barrier, inc=1, device_id=col_dev(lax.rem(c + step, m)), device_id_type=MESH)

    def own_loads(k):
        b = lax.rem(k, 2)
        at = pl.ds(pl.multiple_of(k * CHUNK, CHUNK), CHUNK)
        return (pltpu.make_async_copy(adj_ref.at[at], abuf.at[b], a_sem.at[b]),
                pltpu.make_async_copy(em_ref.at[at], ebuf.at[b], e_sem.at[b]))

    def start_loads(k):
        for copy in own_loads(k):
            copy.start()

    start_loads(0)
    load = pltpu.make_async_copy(fwd_ref, f.at[pl.ds(pl.multiple_of(c * shard, CHUNK), shard)], load_sem)
    load.start()

    def own_block(k):
        @pl.when(k + 1 < chunks)
        def _():
            start_loads(k + 1)

        for copy in own_loads(k):
            copy.wait()
        b = lax.rem(k, 2)
        one_hot = jnp.where(
            idx_ref[...] == lax.broadcasted_iota(jnp.int32, (symbols, positions), 0), 1.0, 0.0
        ).astype(jnp.bfloat16)
        looked = jnp.dot(ebuf[b], one_hot, preferred_element_type=jnp.float32)
        block = abuf[b].astype(jnp.float32) * looked
        w[p * chunks + k] = block.T.astype(jnp.bfloat16)

    own_block(jnp.int32(0))
    pl.semaphore_wait(barrier, jnp.where(p > 0, 1, 0) + jnp.where(p < n - 1, 1, 0) + (m - 1))

    def send_own(k, _):
        @pl.when(k > 0)
        def _():
            own_block(k)

        i = p * chunks + k

        @pl.when(p > 0)
        def _():
            w_copy(i, w_left, p - 1).start()

        @pl.when(p < n - 1)
        def _():
            w_copy(i, w_right, p + 1).start()

        @pl.when(k == 0)
        def _():
            load.wait()

            def send_forward(kf, _):
                j = c * chunks + kf

                @pl.when(c > 0)
                def _():
                    f_copy(j, f_left, c - 1).start()

                @pl.when(c < m - 1)
                def _():
                    f_copy(j, f_right, c + 1).start()

                return 0

            lax.fori_loop(0, chunks, send_forward, 0)

        return 0

    lax.fori_loop(0, chunks, send_own, 0)

    def w_arrive(slot, k):
        i = slot * chunks + k

        @pl.when((slot >= 0) & (slot < n))
        def _():
            w_copy(i, w_left, p).wait_recv()

            @pl.when((slot < p) & (p < n - 1))
            def _():
                w_copy(i, w_right, p + 1).start()

            @pl.when((slot > p) & (p > 0))
            def _():
                w_copy(i, w_left, p - 1).start()

    def f_arrive(slot, k):
        i = slot * chunks + k

        @pl.when((slot >= 0) & (slot < m))
        def _():
            f_copy(i, f_left, c).wait_recv()

            @pl.when((slot < c) & (c < m - 1))
            def _():
                f_copy(i, f_right, c + 1).start()

            @pl.when((slot > c) & (c > 0))
            def _():
                f_copy(i, f_left, c - 1).start()

    def gather(step, _):
        d = 1 + step // chunks
        k = lax.rem(step, chunks)
        f_arrive(c - d, k)
        f_arrive(c + d, k)

        @pl.when(d == m - 1)
        def _():
            w_arrive(p - 1, k)
            w_arrive(p + 1, k)

        return 0

    acc[...] = jnp.zeros_like(acc)
    lax.fori_loop(0, (m - 1) * chunks, gather, 0)

    both = jnp.minimum(p, n - 1 - p)

    def slot_of(o):
        near = (o + 1) // 2
        near_slot = jnp.where(lax.rem(o, 2) == 1, p - near, p + near)
        far = o - both
        far_slot = jnp.where(p > n - 1 - p, p - far, p + far)
        return jnp.where(o <= 2 * both, near_slot, far_slot)

    def columns(q):
        i = slot_of(q // chunks) * chunks + lax.rem(q, chunks)
        return pl.ds(pl.multiple_of(i * CHUNK, CHUNK), CHUNK)

    def t_copy(q):
        b = lax.rem(q, 2)
        return pltpu.make_async_copy(trans_ref.at[:, columns(q)], tbuf.at[b], t_sem.at[b])

    t_copy(0).start()

    def block(q, _):
        slot = slot_of(q // chunks)
        k = lax.rem(q, chunks)
        b = lax.rem(q, 2)

        @pl.when(q + 1 < n * chunks)
        def _():
            t_copy(q + 1).start()

        @pl.when(jnp.abs(slot - p) > 1)
        def _():
            w_arrive(slot, k)

        t_copy(q).wait()
        i = slot * chunks + k

        def tile(r, _):
            at = pl.ds(pl.multiple_of(r * ROWS, ROWS), ROWS)
            counts = jnp.dot(f[at, :], w[i], preferred_element_type=jnp.float32)
            scaled = counts * tbuf[b, at, :].astype(jnp.float32)
            scaled_ref[at, columns(q)] = scaled.astype(jnp.bfloat16)
            part = scaled[:, :128]
            for g in range(1, CHUNK // 128):
                part = part + scaled[:, g * 128:(g + 1) * 128]
            acc[at, :] += part
            return 0

        lax.fori_loop(0, rows // ROWS, tile, 0)
        return 0

    lax.fori_loop(0, n * chunks, block, 0)

    def reduce(r, _):
        at = pl.ds(pl.multiple_of(r * ROWS, ROWS), ROWS)
        tot[c, :, at] = jnp.sum(acc[at, :].T, axis=0, keepdims=True)
        return 0

    lax.fori_loop(0, rows // ROWS, reduce, 0)

    def tot_copy(src, send, dev):
        return pltpu.make_async_remote_copy(
            src_ref=tot.at[src], dst_ref=tot.at[src], send_sem=tot_send.at[send], recv_sem=tot_recv.at[src],
            device_id=col_dev(dev), device_id_type=MESH)

    for step in range(1, m):
        tot_copy(c, step, lax.rem(c + step, m)).start()
    for step in range(1, m):
        tot_copy(lax.rem(c + step, m), step, c).wait_recv()
    factor_ref[...] = states / jnp.sum(tot[...], axis=0)
    for step in range(1, m):
        tot_copy(c, step, lax.rem(c + step, m)).wait_send()

    def sent(i, _):
        slot = i // chunks

        @pl.when((slot >= p) & (p > 0))
        def _():
            w_copy(i, w_left, p - 1).wait_send()

        @pl.when((slot <= p) & (p < n - 1))
        def _():
            w_copy(i, w_right, p + 1).wait_send()

        return 0

    lax.fori_loop(0, n * chunks, sent, 0)

    def f_sent(i, _):
        slot = i // chunks

        @pl.when((slot >= c) & (c > 0))
        def _():
            f_copy(i, f_left, c - 1).wait_send()

        @pl.when((slot <= c) & (c < m - 1))
        def _():
            f_copy(i, f_right, c + 1).wait_send()

        return 0

    lax.fori_loop(0, m * chunks, f_sent, 0)


def fused(n, m, forward, adjoint, emission, emit_index, transition):
    rows, cols = transition.shape
    shard, positions = forward.shape
    chunks = shard // CHUNK
    vmem = pl.BlockSpec(memory_space=pltpu.VMEM)
    anywhere = pl.BlockSpec(memory_space=pl.ANY)
    dma = pltpu.SemaphoreType.DMA
    scaled, factor = pl.pallas_call(
        functools.partial(kernel, n, m, float(cols * m)),
        out_shape=(
            pltpu.VMEM((rows, cols), jnp.bfloat16),
            jax.ShapeDtypeStruct((1, rows), jnp.float32),
        ),
        in_specs=[vmem, anywhere, anywhere, anywhere, anywhere],
        out_specs=(vmem, vmem),
        scratch_shapes=[
            pltpu.VMEM((n * chunks, positions, CHUNK), jnp.bfloat16),
            pltpu.VMEM((rows, positions), jnp.bfloat16),
            pltpu.VMEM((2, CHUNK, positions), jnp.bfloat16),
            pltpu.VMEM((2, CHUNK, emission.shape[1]), jnp.bfloat16),
            pltpu.VMEM((2, rows, CHUNK), jnp.bfloat16),
            pltpu.VMEM((rows, 128), jnp.float32),
            pltpu.VMEM((m, 1, rows), jnp.float32),
            dma((n * chunks,)), dma((n * chunks,)), dma((n * chunks,)),
            dma((m * chunks,)), dma((m * chunks,)), dma((m * chunks,)),
            dma((2,)), dma((2,)), dma((2,)), dma((m,)), dma((m,)), dma,
        ],
        compiler_params=pltpu.CompilerParams(
            collective_id=0, has_side_effects=True, vmem_limit_bytes=29 * 1024 * 1024),
        cost_estimate=pl.CostEstimate(
            flops=2 * rows * cols * positions, bytes_accessed=4 * rows * cols, transcendentals=0),
        name="counts_gather",
    )(emit_index.reshape(1, -1), emission, adjoint, forward, transition)
    return (scaled.astype(jnp.float32) * factor.reshape(rows, 1)).astype(jnp.bfloat16)


def plain(m, forward, adjoint, emission, emit_index, transition):
    symbols = emission.shape[1]
    one_hot = (emit_index[None, :] == lax.iota(jnp.int32, symbols)[:, None]).astype(jnp.bfloat16)
    looked = jnp.dot(emission, one_hot, preferred_element_type=jnp.float32)
    weighted = (adjoint.astype(jnp.float32) * looked).astype(jnp.bfloat16)
    sources = lax.all_gather(forward, "col", axis=0, tiled=True)
    targets = lax.all_gather(weighted, "row", axis=0, tiled=True)
    counts = lax.dot_general(sources, targets, (((1,), (1,)), ((), ())), preferred_element_type=jnp.float32)
    scaled = counts * transition.astype(jnp.float32)
    total = lax.psum(jnp.sum(scaled, axis=1), "col")
    return (scaled * (m * transition.shape[1] / total)[:, None]).astype(jnp.bfloat16)


def solution(mesh):
    n, m = mesh.shape["row"], mesh.shape["col"]

    def body(forward, adjoint, emission, emit_index, transition):
        args = (forward, adjoint, emission, emit_index, transition)
        if n > 2 and m > 1 and forward.shape[0] % CHUNK == 0:
            return fused(n, m, *args)
        return plain(m, *args)

    return jax.shard_map(
        body,
        mesh=mesh,
        in_specs=(
            P(("groups", "row", "col"), None),
            P(("groups", "col", "row"), None),
            P(("col", "row"), None),
            P("groups"),
            P("row", "col"),
        ),
        out_specs=P(("groups", "row"), "col"),
        check_vma=False,
    )
```

```python
import functools

import jax
import jax.numpy as jnp
from jax import lax
from jax.experimental import pallas as pl
from jax.experimental.pallas import tpu as pltpu
from jax.sharding import PartitionSpec as P

CHUNK = 256
ROWS = 1024
MESH = pl.DeviceIdType.MESH


def kernel(n, m, states, idx_ref, em_ref, adj_ref, fwd_ref, trans_ref,
           scaled_ref, factor_ref,
           w, f, abuf, ebuf, tbuf, obuf, acc, tot,
           w_recv, w_right, w_left, f_recv, f_right, f_left,
           a_sem, e_sem, t_sem, o_sem, tot_send, tot_recv, load_sem):
    groups = lax.axis_index("groups")
    p = lax.axis_index("row")
    c = lax.axis_index("col")
    shard = adj_ref.shape[0]
    chunks = shard // CHUNK
    rows = f.shape[0]
    symbols = em_ref.shape[1]
    positions = adj_ref.shape[1]

    def row_dev(q):
        return (groups, q, c)

    def col_dev(q):
        return (groups, p, q)

    def w_copy(i, sem, dev):
        return pltpu.make_async_remote_copy(
            src_ref=w.at[i], dst_ref=w.at[i], send_sem=sem.at[i], recv_sem=w_recv.at[i],
            device_id=row_dev(dev), device_id_type=MESH)

    def f_slice(i):
        return f.at[pl.ds(pl.multiple_of(i * CHUNK, CHUNK), CHUNK)]

    def f_copy(i, sem, dev):
        return pltpu.make_async_remote_copy(
            src_ref=f_slice(i), dst_ref=f_slice(i), send_sem=sem.at[i], recv_sem=f_recv.at[i],
            device_id=col_dev(dev), device_id_type=MESH)

    barrier = pltpu.get_barrier_semaphore()

    @pl.when(p > 0)
    def _():
        pl.semaphore_signal(barrier, inc=1, device_id=row_dev(p - 1), device_id_type=MESH)

    @pl.when(p < n - 1)
    def _():
        pl.semaphore_signal(barrier, inc=1, device_id=row_dev(p + 1), device_id_type=MESH)

    for step in range(1, m):
        pl.semaphore_signal(barrier, inc=1, device_id=col_dev(lax.rem(c + step, m)), device_id_type=MESH)

    def own_loads(k):
        b = lax.rem(k, 2)
        at = pl.ds(pl.multiple_of(k * CHUNK, CHUNK), CHUNK)
        return (pltpu.make_async_copy(adj_ref.at[at], abuf.at[b], a_sem.at[b]),
                pltpu.make_async_copy(em_ref.at[at], ebuf.at[b], e_sem.at[b]))

    def start_loads(k):
        for copy in own_loads(k):
            copy.start()

    start_loads(0)
    load = pltpu.make_async_copy(fwd_ref, f.at[pl.ds(pl.multiple_of(c * shard, CHUNK), shard)], load_sem)
    load.start()

    def own_block(k):
        @pl.when(k + 1 < chunks)
        def _():
            start_loads(k + 1)

        for copy in own_loads(k):
            copy.wait()
        b = lax.rem(k, 2)
        one_hot = jnp.where(
            idx_ref[...] == lax.broadcasted_iota(jnp.int32, (symbols, positions), 0), 1.0, 0.0
        ).astype(jnp.bfloat16)
        looked = jnp.dot(ebuf[b], one_hot, preferred_element_type=jnp.float32)
        block = abuf[b].astype(jnp.float32) * looked
        w[p * chunks + k] = block.T.astype(jnp.bfloat16)

    own_block(jnp.int32(0))
    pl.semaphore_wait(barrier, jnp.where(p > 0, 1, 0) + jnp.where(p < n - 1, 1, 0) + (m - 1))

    def send_own(k, _):
        @pl.when(k > 0)
        def _():
            own_block(k)

        i = p * chunks + k

        @pl.when(p > 0)
        def _():
            w_copy(i, w_left, p - 1).start()

        @pl.when(p < n - 1)
        def _():
            w_copy(i, w_right, p + 1).start()

        @pl.when(k == 0)
        def _():
            load.wait()

            def send_forward(kf, _):
                j = c * chunks + kf

                @pl.when(c > 0)
                def _():
                    f_copy(j, f_left, c - 1).start()

                @pl.when(c < m - 1)
                def _():
                    f_copy(j, f_right, c + 1).start()

                return 0

            lax.fori_loop(0, chunks, send_forward, 0)

        return 0

    lax.fori_loop(0, chunks, send_own, 0)

    def w_arrive(slot, k):
        i = slot * chunks + k

        @pl.when((slot >= 0) & (slot < n))
        def _():
            w_copy(i, w_left, p).wait_recv()

            @pl.when((slot < p) & (p < n - 1))
            def _():
                w_copy(i, w_right, p + 1).start()

            @pl.when((slot > p) & (p > 0))
            def _():
                w_copy(i, w_left, p - 1).start()

    def f_arrive(slot, k):
        i = slot * chunks + k

        @pl.when((slot >= 0) & (slot < m))
        def _():
            f_copy(i, f_left, c).wait_recv()

            @pl.when((slot < c) & (c < m - 1))
            def _():
                f_copy(i, f_right, c + 1).start()

            @pl.when((slot > c) & (c > 0))
            def _():
                f_copy(i, f_left, c - 1).start()

    def gather(step, _):
        d = 1 + step // chunks
        k = lax.rem(step, chunks)
        f_arrive(c - d, k)
        f_arrive(c + d, k)

        @pl.when(d == m - 1)
        def _():
            w_arrive(p - 1, k)
            w_arrive(p + 1, k)

        return 0

    acc[...] = jnp.zeros_like(acc)
    lax.fori_loop(0, (m - 1) * chunks, gather, 0)

    both = jnp.minimum(p, n - 1 - p)

    def slot_of(o):
        near = (o + 1) // 2
        near_slot = jnp.where(lax.rem(o, 2) == 1, p - near, p + near)
        far = o - both
        far_slot = jnp.where(p > n - 1 - p, p - far, p + far)
        return jnp.where(o <= 2 * both, near_slot, far_slot)

    def columns(q):
        i = slot_of(q // chunks) * chunks + lax.rem(q, chunks)
        return pl.ds(pl.multiple_of(i * CHUNK, CHUNK), CHUNK)

    def t_copy(q):
        b = lax.rem(q, 2)
        return pltpu.make_async_copy(trans_ref.at[:, columns(q)], tbuf.at[b], t_sem.at[b])

    def o_copy(q):
        b = lax.rem(q, 2)
        return pltpu.make_async_copy(obuf.at[b], scaled_ref.at[:, columns(q)], o_sem.at[b])

    t_copy(0).start()

    def block(q, _):
        slot = slot_of(q // chunks)
        k = lax.rem(q, chunks)
        b = lax.rem(q, 2)

        @pl.when(q + 1 < n * chunks)
        def _():
            t_copy(q + 1).start()

        @pl.when(jnp.abs(slot - p) > 1)
        def _():
            w_arrive(slot, k)

        @pl.when(q >= 2)
        def _():
            o_copy(q - 2).wait()

        t_copy(q).wait()
        i = slot * chunks + k

        def tile(r, _):
            at = pl.ds(pl.multiple_of(r * ROWS, ROWS), ROWS)
            counts = jnp.dot(f[at, :], w[i], preferred_element_type=jnp.float32)
            scaled = counts * tbuf[b, at, :].astype(jnp.float32)
            obuf[b, at, :] = scaled.astype(jnp.bfloat16)
            part = scaled[:, :128]
            for g in range(1, CHUNK // 128):
                part = part + scaled[:, g * 128:(g + 1) * 128]
            acc[at, :] += part
            return 0

        lax.fori_loop(0, rows // ROWS, tile, 0)
        o_copy(q).start()
        return 0

    lax.fori_loop(0, n * chunks, block, 0)

    def reduce(r, _):
        at = pl.ds(pl.multiple_of(r * ROWS, ROWS), ROWS)
        tot[c, :, at] = jnp.sum(acc[at, :].T, axis=0, keepdims=True)
        return 0

    lax.fori_loop(0, rows // ROWS, reduce, 0)

    def tot_copy(src, send, dev):
        return pltpu.make_async_remote_copy(
            src_ref=tot.at[src], dst_ref=tot.at[src], send_sem=tot_send.at[send], recv_sem=tot_recv.at[src],
            device_id=col_dev(dev), device_id_type=MESH)

    for step in range(1, m):
        tot_copy(c, step, lax.rem(c + step, m)).start()
    o_copy(n * chunks - 2).wait()
    o_copy(n * chunks - 1).wait()
    for step in range(1, m):
        tot_copy(lax.rem(c + step, m), step, c).wait_recv()
    factor_ref[...] = states / jnp.sum(tot[...], axis=0)
    for step in range(1, m):
        tot_copy(c, step, lax.rem(c + step, m)).wait_send()

    def sent(i, _):
        slot = i // chunks

        @pl.when((slot >= p) & (p > 0))
        def _():
            w_copy(i, w_left, p - 1).wait_send()

        @pl.when((slot <= p) & (p < n - 1))
        def _():
            w_copy(i, w_right, p + 1).wait_send()

        return 0

    lax.fori_loop(0, n * chunks, sent, 0)

    def f_sent(i, _):
        slot = i // chunks

        @pl.when((slot >= c) & (c > 0))
        def _():
            f_copy(i, f_left, c - 1).wait_send()

        @pl.when((slot <= c) & (c < m - 1))
        def _():
            f_copy(i, f_right, c + 1).wait_send()

        return 0

    lax.fori_loop(0, m * chunks, f_sent, 0)


def fused(n, m, forward, adjoint, emission, emit_index, transition):
    rows, cols = transition.shape
    shard, positions = forward.shape
    chunks = shard // CHUNK
    vmem = pl.BlockSpec(memory_space=pltpu.VMEM)
    anywhere = pl.BlockSpec(memory_space=pl.ANY)
    dma = pltpu.SemaphoreType.DMA
    scaled, factor = pl.pallas_call(
        functools.partial(kernel, n, m, float(cols * m)),
        out_shape=(
            jax.ShapeDtypeStruct((rows, cols), jnp.bfloat16),
            jax.ShapeDtypeStruct((1, rows), jnp.float32),
        ),
        in_specs=[vmem, anywhere, anywhere, anywhere, anywhere],
        out_specs=(anywhere, vmem),
        scratch_shapes=[
            pltpu.VMEM((n * chunks, positions, CHUNK), jnp.bfloat16),
            pltpu.VMEM((rows, positions), jnp.bfloat16),
            pltpu.VMEM((2, CHUNK, positions), jnp.bfloat16),
            pltpu.VMEM((2, CHUNK, emission.shape[1]), jnp.bfloat16),
            pltpu.VMEM((2, rows, CHUNK), jnp.bfloat16),
            pltpu.VMEM((2, rows, CHUNK), jnp.bfloat16),
            pltpu.VMEM((rows, 128), jnp.float32),
            pltpu.VMEM((m, 1, rows), jnp.float32),
            dma((n * chunks,)), dma((n * chunks,)), dma((n * chunks,)),
            dma((m * chunks,)), dma((m * chunks,)), dma((m * chunks,)),
            dma((2,)), dma((2,)), dma((2,)), dma((2,)), dma((m,)), dma((m,)), dma,
        ],
        compiler_params=pltpu.CompilerParams(
            collective_id=0, has_side_effects=True, vmem_limit_bytes=60 * 1024 * 1024),
        cost_estimate=pl.CostEstimate(
            flops=2 * rows * cols * positions, bytes_accessed=4 * rows * cols, transcendentals=0),
        name="counts_gather",
    )(emit_index.reshape(1, -1), emission, adjoint, forward, transition)
    return (scaled.astype(jnp.float32) * factor.reshape(rows, 1)).astype(jnp.bfloat16)


def plain(m, forward, adjoint, emission, emit_index, transition):
    symbols = emission.shape[1]
    one_hot = (emit_index[None, :] == lax.iota(jnp.int32, symbols)[:, None]).astype(jnp.bfloat16)
    looked = jnp.dot(emission, one_hot, preferred_element_type=jnp.float32)
    weighted = (adjoint.astype(jnp.float32) * looked).astype(jnp.bfloat16)
    sources = lax.all_gather(forward, "col", axis=0, tiled=True)
    targets = lax.all_gather(weighted, "row", axis=0, tiled=True)
    counts = lax.dot_general(sources, targets, (((1,), (1,)), ((), ())), preferred_element_type=jnp.float32)
    scaled = counts * transition.astype(jnp.float32)
    total = lax.psum(jnp.sum(scaled, axis=1), "col")
    return (scaled * (m * transition.shape[1] / total)[:, None]).astype(jnp.bfloat16)


def solution(mesh):
    n, m = mesh.shape["row"], mesh.shape["col"]

    def body(forward, adjoint, emission, emit_index, transition):
        args = (forward, adjoint, emission, emit_index, transition)
        tiled = forward.shape[0] % CHUNK == 0 and transition.shape[0] % ROWS == 0
        if n > 2 and m > 1 and tiled:
            return fused(n, m, *args)
        return plain(m, *args)

    return jax.shard_map(
        body,
        mesh=mesh,
        in_specs=(
            P(("groups", "row", "col"), None),
            P(("groups", "col", "row"), None),
            P(("col", "row"), None),
            P("groups"),
            P("row", "col"),
        ),
        out_specs=P(("groups", "row"), "col"),
        check_vma=False,
    )
```
